128 devices in a mesh: gx: 8 (over y, z_hi), gy: 4 (over x), gz: 4 (over z_lo, core).
Axes of the slice: x: 4, y: 4, z: 4 (z_hi: 2, z_lo: 2; z = z_hi * 2 + z_lo), core: 2. Of those that a mesh axis runs over, the one named last changes fastest.
Arguments:
- concentrations: float32 [2, 256, 256, 512], P(None, 'gx', 'gy', 'gz'), may hold values from 0 to 2
- pore: int32 [256, 256, 512], P('gx', 'gy', 'gz'), may hold values 0 or 1
- permeability: float32 [256, 256, 512], P('gx', 'gy', 'gz'), may hold values from 0.85 to 1
- rate: float32 [256, 256, 512], P('gx', 'gy', 'gz'), may hold values from 0.01 to 0.1
- diffusion: float32 [2], replicated, may hold values from 0.14 to 0.16
Outputs:
- final: float32 [2, 256, 256, 512], P(None, 'gx', 'gy', 'gz')
The draws below stay inside these ranges and needn't reach their ends.
All inputs are finite; a program needn't handle non-finite values. No bound on the sum of `pore` on one device may be relied on, other than what follows from the above.
Results may differ from the reference program's by a relative error of at most 0.00002.
Values sent between devices are 32-bit elements; how exact they have to be, the bound alone decides.
No kernel may reach another device: no remote copies, remote signals or barrier semaphores. Data moves between devices by JAX's collectives and lax.ppermute only.
A program may use at most 128 MiB of HBM per device.

```python
import math
import jax
import jax.numpy as jnp

STEPS = 16
NX = 256
NY = 256
NZ = 512


def draw_concentrations(key, part):
    key = jax.random.fold_in(key, 11)
    shape = (2, NX, NY, NZ)
    return jax.random.uniform(key, shape, jnp.float32, 0.0, 2.0)


def with_ends(drawn, rng, smallest, high):
    index_at = [jax.random.randint(jax.random.fold_in(rng, axis), (), 0, length) for axis, length in enumerate(drawn.shape)]
    widest = drawn.shape.index(max(drawn.shape))
    neighbour = index_at[:widest] + [(index_at[widest] + 1) % drawn.shape[widest]] + index_at[widest + 1:]
    return drawn.at[tuple(index_at)].set(smallest).at[tuple(neighbour)].set(high)


def shard_levels(stream_key, extent, shards, low, largest):
    gain, own = 1.0, jax.random.fold_in(stream_key, 6)
    for dim, shards_of in shards:
        steps = jnp.exp(jax.random.uniform(jax.random.fold_in(own, dim), (shards_of,), jnp.float32, low / len(shards), largest / len(shards)))
        gain = gain * jnp.repeat(steps, extent[dim] // shards_of).reshape([-1 if axis == dim else 1 for axis in range(len(extent))])
    return gain


def setup_inputs(seed: int = 0) -> dict:
    splits = jax.random.split(jax.random.key(seed), 6)
    return {
        "concentrations": draw_concentrations(jax.random.fold_in(splits[5], 71), 0),
        "pore": with_ends((jax.random.randint(splits[1], (NX, NY, NZ), 0, 32) < 31).astype(jnp.int32), jax.random.fold_in(splits[1], 1), 0, 1),
        "permeability": jnp.clip(0.85 + 0.14999998 * jax.random.uniform(splits[2], (NX, NY, NZ), jnp.float32) ** shard_levels(splits[2], (NX, NY, NZ), ((0, 8), (1, 4), (2, 4)), -0.2, 0.2), 0.85, 1.0),
        "rate": jnp.clip(jnp.exp(math.log(0.1) - 2.3025851 * jax.random.uniform(splits[3], (NX, NY, NZ), jnp.float32) ** shard_levels(splits[3], (NX, NY, NZ), ((0, 8), (1, 4), (2, 4)), -0.2, 0.2)), 0.01, 0.1),
        "diffusion": jnp.clip(jax.random.uniform(splits[4], (2,), jnp.float32, 0.14, 0.16), 0.14, 0.16),
    }


def advance(fields, rock, diffusion):
    conduct = rock[0]
    react = rock[1]
    center = fields[:, 1:-1, 1:-1, 1:-1]
    kc = conduct[1:-1, 1:-1, 1:-1]
    flux = jnp.zeros_like(center)
    for shift_x, shift_y, shift_z in ((0, 1, 1), (2, 1, 1), (1, 0, 1), (1, 2, 1), (1, 1, 0), (1, 1, 2)):
        size_x = fields.shape[1] - 2
        size_y = fields.shape[2] - 2
        size_z = fields.shape[3] - 2
        near = fields[:, shift_x:shift_x + size_x, shift_y:shift_y + size_y, shift_z:shift_z + size_z]
        near_k = conduct[shift_x:shift_x + size_x, shift_y:shift_y + size_y, shift_z:shift_z + size_z]
        flux = flux + near_k[None] * (near - center)
    flux = kc[None] * flux
    acid = center[0]
    reacted = react[1:-1, 1:-1, 1:-1] * acid * acid / (1.0 + acid)
    new_acid = acid + diffusion[0] * flux[0] - reacted
    new_solute = center[1] + diffusion[1] * flux[1] + reacted
    return jnp.stack([new_acid, new_solute])


def reference(concentrations, pore, permeability, rate, diffusion):
    solid = pore.astype(jnp.float32)
    rock = jnp.stack([solid * permeability, solid * rate])
    rock = jnp.pad(rock, ((0, 0), (1, 1), (1, 1), (1, 1)))
    fields = concentrations
    for step in range(STEPS):
        padded = jnp.pad(fields, ((0, 0), (1, 1), (1, 1), (1, 1)))
        fields = advance(padded, rock, diffusion)
    return fields
```

```python
import functools

import jax
import jax.numpy as jnp
from jax import lax
from jax.experimental import pallas as pl
from jax.experimental.pallas import tpu as pltpu
from jax.sharding import PartitionSpec as P

STEPS = 16
DEEP = 4
NX, NY, NZ = 32, 64, 128
XF = NX + 2 * DEEP
YF = NY + 32
ROW = 16
GROUP, GROUP_DOT, GROUP_STRIPS = 2, 20, 8
TILES = NY // 8 + 2
VMEM = pl.BlockSpec(memory_space=pltpu.VMEM)
SMEM = pl.BlockSpec(memory_space=pltpu.SMEM)
LIMIT = 48 * 1024 * 1024


def lanes():
    return lax.broadcasted_iota(jnp.int32, (8, 128), 1)


def rows():
    return lax.broadcasted_iota(jnp.int32, (8, 128), 0)


def roll(tile, shift, axis=1):
    size = tile.shape[axis]
    shift = shift % size
    return pltpu.roll(tile, shift, axis) if shift else tile


def ring(block, axis, distance):
    size = lax.axis_size(axis)
    return lax.ppermute(block, axis, [(i, (i + distance) % size) for i in range(size)])


def split(block, terms):
    parts = []
    for _ in range(terms):
        part = block.astype(jnp.bfloat16)
        block = block - part.astype(jnp.float32)
        parts.append(part)
    return jnp.concatenate(parts, axis=-1)


def zeros_and_ones(kind, terms):
    i = lax.broadcasted_iota(jnp.int32, (128, 128), 0)
    j = lax.broadcasted_iota(jnp.int32, (128, 128), 1)
    ones = (i == j + 1) | (i + 1 == j) if kind == "near" else i == (j ^ 7)
    return jnp.concatenate([jnp.where(ones, 1.0, 0.0).astype(jnp.bfloat16)] * terms, axis=0)


def pack_strips(edges, right, left, fields, skip):
    low = (lanes() & 7) < 4
    half = NX // 2
    back = zeros_and_ones("turn", 3)
    for f in range(fields):
        turned = jnp.dot(
            split(edges[f, skip : skip + NX].reshape(NX * 8, 128), 3), back, preferred_element_type=jnp.float32
        ).reshape(NX, 8, 128)
        for x in range(half):
            near, far = turned[x], turned[x + half]
            right[f, x] = jnp.where(low, roll(far, -4), near)
            left[f, x] = jnp.where(low, near, roll(far, 4))


def prepare(conc, pore, perm, rate, fields, xlo, xhi, right, left, edges):
    lane = lanes()

    def plane(x):
        strip = [jnp.zeros((8, 128), jnp.float32)] * 4
        for t in range(1, 9):
            here = pl.ds(8 * (t - 1), 8)
            solid = pore[x, here, :].astype(jnp.float32)
            k = solid * perm[x, here, :]
            r = solid * rate[x, here, :]
            for f, value in enumerate((k * conc[0, x, here, :], k * conc[1, x, here, :], k, r)):
                fields[f, x, here, :] = value
                strip[f] = jnp.where((lane >> 3) == t, roll(value, 8 * t + 4), strip[f])
        for f in range(4):
            edges[f, x] = strip[f]

    grouped(0, NX, GROUP, plane)
    for f in range(4):
        xlo[f] = fields[f, 0:DEEP]
        xhi[f] = fields[f, NX - DEEP : NX]
    pack_strips(edges, right, left, 4, 0)


def strips_in(flags, fields, from_left, from_right, strips, ylo, yhi, *, count):
    lane, row = lanes(), rows()
    low = (lane & 7) < 4
    left_ok, right_ok = flags[4], flags[5]
    half = NX // 2
    for f in range(count):

        for x in range(half):
            before, after = from_left[f, x] * left_ok, from_right[f, x] * right_ok
            strips[f, x] = jnp.where(low, after, before)
            strips[f, x + half] = jnp.where(low, roll(after, -4), roll(before, 4))
        for x in range(NX):
            ylo[f, x] = fields[f, x, 0:4, :]
            yhi[f, x] = fields[f, x, NY - 4 : NY, :]
        for group in range(2):
            first = jnp.zeros((8, 128), jnp.float32)
            last = first
            for i in range(16):
                strip = strips[f, group * 16 + i]
                mine = (lane >> 3) == i
                first = jnp.where(mine, roll(strip, 8 * i - 8), first)
                last = jnp.where(mine, roll(strip, 8 * i - 64), last)
            ylo[f, NX + group] = first[0:4]
            yhi[f, NX + group] = last[4:8]


def strips_all(flags, own, from_low, from_high, strips, elo, ehi, *, count):
    lane, row = lanes(), rows()
    low_ok, high_ok = flags[2], flags[3]
    under = (lane < 8) & (row >= 4)
    over = ((lane >> 3) == 9) & (row < 4)
    for f in range(count):
        for group in range(2):
            below = from_low[f, NX + group] * low_ok
            above = from_high[f, NX + group] * high_ok
            below = jnp.concatenate([below, below], axis=0)
            above = jnp.concatenate([above, above], axis=0)
            for i in range(16):
                x = group * 16 + i
                strip = jnp.where(under, roll(below, -8 * i), own[f, x])
                strips[f, x] = jnp.where(over, roll(above, 72 - 8 * i), strip)
        for d in range(DEEP):
            for out, x in ((elo, d), (ehi, NX - DEEP + d)):
                out[f, d, 0:4, :] = from_low[f, x] * low_ok
                out[f, d, 4:8, :] = from_high[f, x] * high_ok
                out[f, d, 8:16, :] = strips[f, x]


def assemble(flags, f, main, strip, own, strips, ylo, yhi, xlo, xhi, elo, ehi):
    def plane(x):
        main[x + DEEP, ROW : ROW + NY, :] = own[f, x]
        main[x + DEEP, ROW - 4 : ROW, :] = ylo[f, x] * flags[2]
        main[x + DEEP, ROW + NY : ROW + NY + 4, :] = yhi[f, x] * flags[3]
        strip[x + DEEP] = strips[f, x]

    grouped(0, NX, 4, plane)
    for slab, edge, at, ok in ((xlo, elo, 0, flags[0]), (xhi, ehi, DEEP + NX, flags[1])):
        for d in range(DEEP):
            main[at + d, ROW : ROW + NY, :] = slab[f, d] * ok
            main[at + d, ROW - 4 : ROW, :] = edge[f, d, 0:4, :] * ok
            main[at + d, ROW + NY : ROW + NY + 4, :] = edge[f, d, 4:8, :] * ok
            strip[at + d] = edge[f, d, 8:16, :] * ok


def near_z(main, sums, start, stop, row, rows, near):
    def several(x):
        block = main[pl.ds(x, size), row : row + rows, :].reshape(size * rows, NZ)
        total = jnp.dot(split(block, 2), near, preferred_element_type=jnp.float32)
        sums[pl.ds(x, size)] = total.reshape(size, rows, NZ)

    groups = -(-(stop - start) // GROUP_DOT)
    size = -(-(stop - start) // groups)

    def step(i, _):
        several(jnp.minimum(start + i * size, stop - size))
        return 0

    lax.fori_loop(0, groups, step, 0)


def ends_z(strip, t, ends):
    return jnp.where(ends, roll(strip, -(8 * t + 4)), 0.0)


def near_xy(main, x, t):
    at = 8 + 8 * t
    rows_y = main[x, at - 1 : at + 7, :] + main[x, at + 1 : at + 9, :]
    rows_x = main[x - 1, at : at + 8, :] + main[x + 1, at : at + 8, :]
    return rows_y + rows_x


def near_sum_strip(strip, x, edge, lane, row):
    here = strip[x]
    left = jnp.where((lane & 7) == 4, edge, roll(here, 1))
    right = jnp.where((lane & 7) == 3, edge, roll(here, -1))
    up = roll(here, -1, 0)
    up = jnp.where(row == 7, roll(up, -8), up)
    down = roll(here, 1, 0)
    down = jnp.where(row == 0, roll(down, 8), down)
    return (up + down) + (strip[x - 1] + strip[x + 1]) + (left + right), here


def react_step(d0, d1, u0, u1, s0, s1, k, g, r):
    kk = k * k
    over = jnp.maximum(k + u0, 0.5)
    inverse = pl.reciprocal(over, approx=True)
    inverse = inverse * (2.0 - over * inverse)
    q = (r * u0) * (u0 * inverse)
    n0 = u0 + (d0 * (kk * s0 - g * u0) - q)
    n1 = u1 + (d1 * (kk * s1 - g * u1) + q)
    return n0, n1


def advance(*refs, first, last):
    refs = list(refs)
    take = lambda n: [refs.pop(0) for _ in range(n)]
    flags, diffusion = take(2)
    own, strips, ylo, yhi, xlo, xhi, elo, ehi = halo = take(8)
    if not first:
        k_main, g_main, r_main, k_strip, g_strip, r_strip = take(6)
    if last:
        (conc,) = take(1)
        (out,) = take(1)
    else:
        out, out_xlo, out_xhi, right, left = take(5)
    if first:
        k_main, g_main, r_main, k_strip, g_strip, r_strip = take(6)
    a_main, b_main, a_strip, b_strip, edges, near = take(6)

    lane, row = lanes(), rows()
    zero = jnp.zeros((8, 128), jnp.float32)
    ends = (lane == 0) | (lane == 127)
    beside = zeros_and_ones("near", 2)
    d0, d1 = diffusion[0], diffusion[1]
    for f in range(2):
        assemble(flags, f, a_main.at[f], a_strip.at[f], *halo)
    if first:
        assemble(flags, 2, k_main, k_strip, *halo)
        assemble(flags, 3, r_main, r_strip, *halo)

        near_z(k_main, near.at[0], 1, XF - 1, 8, 8 * TILES, beside)

        def weigh(x):
            edge, strip = zero, k_strip[x]
            for t in range(TILES):
                at = pl.ds(8 + 8 * t, 8)
                here = k_main[x, at, :]
                total = near_xy(k_main, x, t) + (near[0, x, 8 * t : 8 * t + 8, :] + ends_z(strip, t, ends))
                g_main[x, at, :] = here * total
                edge = jnp.where((lane >> 3) == t, roll(here, 8 * t + 4), edge)
            edges[0, x] = edge

        def weigh_strip(x):
            total, here = near_sum_strip(k_strip, x, edges[0, x], lane, row)
            g_strip[x] = here * total

        grouped(1, XF - 1, GROUP, weigh)
        grouped(1, XF - 1, GROUP_STRIPS, weigh_strip)

    for s in range(1, DEEP + 1):
        src, dst = (a_main, b_main) if s % 2 else (b_main, a_main)
        src_strip, dst_strip = (a_strip, b_strip) if s % 2 else (b_strip, a_strip)
        ending = s == DEEP

        tiles = range(1, TILES - 1) if ending else range(TILES)

        def plane(x):
            edge, strip = [zero, zero], [src_strip[0, x], src_strip[1, x]]
            for t in tiles:
                at = pl.ds(8 + 8 * t, 8)
                there = pl.ds(8 * t, 8)
                u0, u1 = src[0, x, at, :], src[1, x, at, :]
                s0 = near_xy(src.at[0], x, t) + (near[0, x, there, :] + ends_z(strip[0], t, ends))
                s1 = near_xy(src.at[1], x, t) + (near[1, x, there, :] + ends_z(strip[1], t, ends))
                k, r = k_main[x, at, :], r_main[x, at, :]
                new = react_step(d0, d1, u0, u1, s0, s1, k, g_main[x, at, :], r)
                for f in range(2):
                    if not ending:
                        dst[f, x, at, :] = new[f]
                        edge[f] = jnp.where((lane >> 3) == t, roll((u0, u1)[f], 8 * t + 4), edge[f])
                    elif last:
                        was = conc[f, x - DEEP, 8 * (t - 1) : 8 * t, :]
                        out[f, x - DEEP, 8 * (t - 1) : 8 * t, :] = jnp.where(k > 0, new[f] / jnp.maximum(k, 0.5), was)
                    else:
                        out[f, x - DEEP, 8 * (t - 1) : 8 * t, :] = new[f]
                        edge[f] = jnp.where((lane >> 3) == t, roll(new[f], 8 * t + 4), edge[f])
            if not (ending and last):
                for f in range(2):
                    edges[f, x] = edge[f]

        def plane_strips(x):
            s0, u0 = near_sum_strip(src_strip.at[0], x, edges[0, x], lane, row)
            s1, u1 = near_sum_strip(src_strip.at[1], x, edges[1, x], lane, row)
            new = react_step(d0, d1, u0, u1, s0, s1, k_strip[x], g_strip[x], r_strip[x])
            for f in range(2):
                dst_strip[f, x] = new[f]

        for f in range(2):
            near_z(src.at[f], near.at[f], s, XF - s, 8, 8 * TILES, beside)
        grouped(s, XF - s, GROUP, plane)
        if not ending:
            grouped(s, XF - s, GROUP_STRIPS, plane_strips)

    if not last:

        for f in range(2):
            out_xlo[f] = out[f, 0:DEEP]
            out_xhi[f] = out[f, NX - DEEP : NX]
        pack_strips(edges, right, left, 2, DEEP)


def grouped(start, stop, size, work):
    def several(i, _):
        first = jnp.minimum(start + i * size, stop - size)
        for j in range(size):
            work(first + j)
        return 0

    lax.fori_loop(0, -(-(stop - start) // size), several, 0)


def call(kernel, outs, scratch, args, smem, name):
    f32 = lambda shape: jax.ShapeDtypeStruct(shape, jnp.float32)
    return pl.pallas_call(
        kernel,
        out_shape=[f32(shape) for shape in outs],
        in_specs=[SMEM] * smem + [VMEM] * (len(args) - smem),
        out_specs=[VMEM] * len(outs),
        scratch_shapes=[pltpu.VMEM(shape, jnp.float32) for shape in scratch],
        compiler_params=pltpu.CompilerParams(vmem_limit_bytes=LIMIT),
        name=name,
    )(*args)


def shards(concentrations, pore, permeability, rate, diffusion):
    place = []
    for axis in ("gx", "gy", "gz"):
        index = lax.axis_index(axis)
        place += [index > 0, index < lax.axis_size(axis) - 1]
    flags = jnp.stack(place).astype(jnp.float32)

    own, xlo, xhi, right, left = call(
        prepare,
        [(4, NX, NY, NZ)] + [(4, DEEP, NY, NZ)] * 2 + [(4, NX // 2, 8, 128)] * 2,
        [(4, NX, 8, 128)],
        (concentrations, pore, permeability, rate),
        0,
        "prepare",
    )
    rock = ()
    rounds = STEPS // DEEP
    for turn in range(rounds):
        first, last = turn == 0, turn == rounds - 1
        count = 4 if first else 2
        from_xlo, from_xhi = ring(xhi, "gx", 1), ring(xlo, "gx", -1)
        from_left, from_right = ring(right, "gz", 1), ring(left, "gz", -1)
        strips, ylo, yhi = call(
            functools.partial(strips_in, count=count),
            [(count, NX, 8, 128)] + [(count, NX + 2, 4, NZ)] * 2,
            [],
            (flags, own, from_left, from_right),
            1,
            "strips_in",
        )
        from_ylo, from_yhi = ring(yhi, "gy", 1), ring(ylo, "gy", -1)
        strips, elo, ehi = call(
            functools.partial(strips_all, count=count),
            [(count, NX, 8, 128)] + [(count, DEEP, 16, NZ)] * 2,
            [],
            (flags, strips, from_ylo, from_yhi),
            1,
            "strips_all",
        )
        from_elo, from_ehi = ring(ehi, "gx", 1), ring(elo, "gx", -1)
        args = (flags, diffusion, own, strips, from_ylo, from_yhi, from_xlo, from_xhi, from_elo, from_ehi, *rock)
        outs = [(2, NX, NY, NZ)]
        if last:
            args += (concentrations,)
        else:
            outs += [(2, DEEP, NY, NZ)] * 2 + [(2, NX // 2, 8, 128)] * 2
        if first:
            outs += [(XF, YF, NZ)] * 3 + [(XF, 8, 128)] * 3
        scratch = [(2, XF, YF, NZ)] * 2 + [(2, XF, 8, 128)] * 3 + [(2, XF, 8 * TILES, NZ)]
        results = call(functools.partial(advance, first=first, last=last), outs, scratch, args, 2, "advance")
        if last:
            return results[0]
        own, xlo, xhi, right, left = results[:5]
        if first:
            rock = tuple(results[5:])


def solution(mesh):
    placed = (
        P(None, "gx", "gy", "gz"),
        P("gx", "gy", "gz"),
        P("gx", "gy", "gz"),
        P("gx", "gy", "gz"),
        P(),
    )
    return jax.shard_map(
        shards, mesh=mesh, in_specs=placed, out_specs=P(None, "gx", "gy", "gz"), check_vma=False
    )
```

```python
import functools

import jax
import jax.numpy as jnp
from jax import lax
from jax.experimental import pallas as pl
from jax.experimental.pallas import tpu as pltpu
from jax.sharding import PartitionSpec as P

STEPS = 16
ROUNDS = (6, 5, 5)
HALO = 6
WIDE = 2 * HALO
NX, NY, NZ = 32, 64, 128
YF = NY + 32
ROW = 16
GROUP_STRIPS = 8
TILES = NY // 8 + 2
VMEM = pl.BlockSpec(memory_space=pltpu.VMEM)
SMEM = pl.BlockSpec(memory_space=pltpu.SMEM)
ANY = pl.BlockSpec(memory_space=pl.ANY)
MIB = 1024 * 1024
OUTER_LIMIT = 28


def lanes():
    return lax.broadcasted_iota(jnp.int32, (8, 128), 1)


def groups():
    lane = lanes()
    group = row_tile(lane)
    return group, lane - WIDE * group


def row_tile(lane):
    return (lane * -(-4096 // WIDE)) >> 12


def rows():
    return lax.broadcasted_iota(jnp.int32, (8, 128), 0)


def roll(tile, shift, axis=1):
    size = tile.shape[axis]
    shift = shift % size
    return pltpu.roll(tile, shift, axis) if shift else tile


def ring(block, axis, distance):
    size = lax.axis_size(axis)
    return lax.ppermute(block, axis, [(i, (i + distance) % size) for i in range(size)])


def split(block, terms):
    parts = []
    for _ in range(terms):
        part = block.astype(jnp.bfloat16)
        block = block - part.astype(jnp.float32)
        parts.append(part)
    return jnp.concatenate(parts, axis=-1)


def zeros_and_ones(kind, terms):
    i = lax.broadcasted_iota(jnp.int32, (128, 128), 0)
    j = lax.broadcasted_iota(jnp.int32, (128, 128), 1)
    ones = (i == j + 1) | (i + 1 == j) if kind == "near" else i + j == 2 * WIDE * row_tile(i) + WIDE - 1
    return jnp.concatenate([jnp.where(ones, 1.0, 0.0).astype(jnp.bfloat16)] * terms, axis=0)


def pack_strips(edges, right, left, fields):
    low = groups()[1] < HALO
    half = NX // 2
    back = zeros_and_ones("turn", 3)
    for f in range(fields):
        turned = jnp.dot(
            split(edges[f].reshape(NX * 8, 128), 3), back, preferred_element_type=jnp.float32
        ).reshape(NX, 8, 128)
        for x in range(half):
            near, far = turned[x], turned[x + half]
            right[f, x] = jnp.where(low, roll(far, -HALO), near)
            left[f, x] = jnp.where(low, near, roll(far, HALO))


SOME = 4


def prepare(conc, pore, perm, rate, fields, xlo, xhi, rock_lo, rock_hi, right, left, rows_lo, rows_hi, edges):
    group = groups()[0]
    deep = ROUNDS[0]
    turn = pl.program_id(0)

    for x in range(SOME):
        strip = [jnp.zeros((8, 128), jnp.float32)] * 4
        for t in range(1, 9):
            here = pl.ds(8 * (t - 1), 8)
            solid = pore[x, here, :].astype(jnp.float32)
            k = solid * perm[x, here, :]
            r = solid * rate[x, here, :]
            for f, value in enumerate((k * conc[0, x, here, :], k * conc[1, x, here, :], k, r)):
                fields[f, x, here, :] = value
                strip[f] = jnp.where(group == t, roll(value, WIDE * t + HALO), strip[f])
        for f in range(4):
            edges[f, SOME * turn + x] = strip[f]
            rows_lo[f, HALO * x : HALO * (x + 1), :] = fields[f, x, 0:HALO, :]
            rows_hi[f, HALO * x : HALO * (x + 1), :] = fields[f, x, NY - HALO : NY, :]

    for out, rock, first in ((xlo, rock_lo, 0), (xhi, rock_hi, NX - deep)):
        for d in range(deep):
            there, here = divmod(first + d, SOME)

            @pl.when(turn == there)
            def _():
                for f in range(2):
                    out[f, d] = fields[f, here]
                    rock[f, d] = fields[f + 2, here]

    @pl.when(turn == NX // SOME - 1)
    def _():
        pack_strips(edges, right, left, 4)


def strips_in(flags, rows_lo, rows_hi, from_left, from_right, strips, ylo, yhi, *, count):
    group, place = groups()
    low = place < HALO
    left_ok, right_ok = flags[4], flags[5]
    half = NX // 2
    for f in range(count):
        for x in range(half):
            before, after = from_left[f, x] * left_ok, from_right[f, x] * right_ok
            strips[f, x] = jnp.where(low, after, before)
            strips[f, x + half] = jnp.where(low, roll(after, -HALO), roll(before, HALO))
        ylo[f, 0 : NX * HALO] = rows_lo[f]
        yhi[f, 0 : NX * HALO] = rows_hi[f]
        for some in range(4):
            first = last = jnp.zeros((8, 128), jnp.float32)
            for i in range(8):
                strip = strips[f, some * 8 + i]
                mine = group == i
                first = jnp.where(mine, roll(strip, WIDE * (i - 1)), first)
                last = jnp.where(mine, roll(strip, WIDE * (i - 8)), last)
            at = NX * HALO + 8 * some
            ylo[f, at : at + 8] = first
            yhi[f, at : at + 8] = last


def message(deep):
    edge = 8 * (deep - 1) + deep * (deep - 1)
    edge = -(-edge // 8) * 8
    at = 8 * (deep - 1)
    parts = []
    for d in range(1, deep + 1):
        more = deep - d
        parts.append((edge + NY * (d - 1), 8 * (d - 1), at, at + more, more))
        at += 2 * more
    return parts, edge, edge + NY * deep


def strips_all(flags, own, from_low, from_high, xlo, xhi, strips, *outs, count, deep):
    group, row = groups()[0], rows()
    low_ok, high_ok = flags[2], flags[3]
    under = (group == 0) & (row >= 8 - HALO)
    over = (group == 9) & (row < HALO)
    for f in range(count):
        for some in range(4):
            at = NX * HALO + 8 * some
            below = from_low[f, at : at + 8] * low_ok
            above = from_high[f, at : at + 8] * high_ok
            for i in range(8):
                x = some * 8 + i
                strip = jnp.where(under, roll(below, -WIDE * i), own[f, x])
                strips[f, x] = jnp.where(over, roll(above, WIDE * (9 - i)), strip)
        for d, (at_own, at_strip, at_below, at_above, more) in enumerate(message(deep)[0], 1):
            for side, slab, x in ((0, xlo, d - 1), (1, xhi, NX - d)):
                out, i = (outs[side], f) if f < 2 else (outs[2 + side], f - 2)
                if f < 2:
                    out[i, at_own : at_own + NY] = slab[f, d - 1 if side == 0 else slab.shape[1] - d]
                if more:
                    out[i, at_strip : at_strip + 8] = strips[f, x]
                    low, high = HALO * (x + 1) - more, HALO * x
                    out[i, at_below : at_below + more] = from_low[f, low : low + more] * low_ok
                    out[i, at_above : at_above + more] = from_high[f, high : high + more] * high_ok


def place_plane(main, strip, to, block, below, above, side):
    if block is not None:
        main[to, ROW : ROW + NY, :] = block
    if below is not None:
        more = below.shape[0]
        main[to, ROW - more : ROW, :] = below
        main[to, ROW + NY : ROW + NY + more, :] = above
        strip[to] = side


def near_z(src, sums, pieces, near):
    blocks = [src[f, pl.ds(x, n), 8 : 8 + 8 * TILES, :].reshape(n * 8 * TILES, NZ) for f, x, n in pieces]
    block = jnp.concatenate(blocks, axis=0) if len(blocks) > 1 else blocks[0]
    total = jnp.dot(split(block, 2), near, preferred_element_type=jnp.float32)
    at = 0
    for f, x, n in pieces:
        sums[f, pl.ds(x, n)] = total[at : at + n * 8 * TILES].reshape(n, 8 * TILES, NZ)
        at += n * 8 * TILES


def ends_z(strip, t, ends):
    return jnp.where(ends, roll(strip, -(WIDE * t + HALO)), 0.0)


def near_xy(main, x, t):
    at = 8 + 8 * t
    rows_y = main[x, at - 1 : at + 7, :] + main[x, at + 1 : at + 9, :]
    rows_x = main[x - 1, at : at + 8, :] + main[x + 1, at : at + 8, :]
    return rows_y + rows_x


def near_sum_strip(strip, x, edge, place, row):
    here = strip[x]
    left = jnp.where(place == HALO, edge, roll(here, 1))
    right = jnp.where(place == HALO - 1, edge, roll(here, -1))
    up = roll(here, -1, 0)
    up = jnp.where(row == 7, roll(up, -WIDE), up)
    down = roll(here, 1, 0)
    down = jnp.where(row == 0, roll(down, WIDE), down)
    return (up + down) + (strip[x - 1] + strip[x + 1]) + (left + right), here


def react_step(d0, d1, u0, u1, s0, s1, k, g, r):
    kk = k * k
    over = jnp.maximum(k + u0, 0.5)
    inverse = pl.reciprocal(over, approx=True)
    inverse = inverse * (2.0 - over * inverse)
    q = (r * u0) * (u0 * inverse)
    n0 = u0 + (d0 * (kk * s0 - g * u0) - q)
    n1 = u1 + (d1 * (kk * s1 - g * u1) + q)
    return n0, n1


class Step:
    def __init__(self, diffusion, rock, near, edges):
        lane, self.row = lanes(), rows()
        self.group, self.place = groups()
        self.zero = jnp.zeros((8, 128), jnp.float32)
        self.ends = (lane == 0) | (lane == 127)
        self.beside = zeros_and_ones("near", 2)
        self.d = diffusion[0], diffusion[1]
        self.k, self.g, self.r, self.k_strip, self.g_strip, self.r_strip = rock
        self.near, self.edges = near, edges

    def into(self, edge, t, tile):
        return jnp.where(self.group == t, roll(tile, WIDE * t + HALO), edge)

    def weigh(self, ranges):
        def plane(x):
            edge, strip = self.zero, self.k_strip[x]
            for t in range(TILES):
                at = pl.ds(8 + 8 * t, 8)
                here = self.k[x, at, :]
                total = near_xy(self.k, x, t) + (self.near[0, x, 8 * t : 8 * t + 8, :] + ends_z(strip, t, self.ends))
                self.g[x, at, :] = here * total
                edge = self.into(edge, t, here)
            self.edges[0, x] = edge

        def side(x):
            total, here = near_sum_strip(self.k_strip, x, self.edges[0, x], self.place, self.row)
            self.g_strip[x] = here * total

        for start, stop in ranges:
            near_z(Only(self.k), self.near, [(0, start, stop - start)], self.beside)
            grouped(start, stop, group_of(stop - start), plane)
            grouped(start, stop, GROUP_STRIPS, side)

    def run(self, src, src_strip, ranges, dots, write, write_strip=None, ready=None):
        tiles = range(TILES) if write_strip else range(1, TILES - 1)
        for pieces in dots:
            near_z(src, self.near, pieces, self.beside)
        if ready:
            ready()

        def plane(x):
            edge, strip = [self.zero] * 2, [src_strip[0, x], src_strip[1, x]]
            for t in tiles:
                at = pl.ds(8 + 8 * t, 8)
                u = [src[f, x, at, :] for f in range(2)]
                total = [
                    near_xy(src.at[f], x, t) + (self.near[f, x, 8 * t : 8 * t + 8, :] + ends_z(strip[f], t, self.ends))
                    for f in range(2)
                ]
                k = self.k[x, at, :]
                new = react_step(*self.d, *u, *total, k, self.g[x, at, :], self.r[x, at, :])
                write(x, t, new, k)
                for f in range(2):
                    edge[f] = self.into(edge[f], t, u[f] if write_strip else new[f])
            for f in range(2):
                self.edges[f, x] = edge[f]

        def side(x):
            both = [near_sum_strip(src_strip.at[f], x, self.edges[f, x], self.place, self.row) for f in range(2)]
            total, u = zip(*both)
            write_strip(x, react_step(*self.d, *u, *total, self.k_strip[x], self.g_strip[x], self.r_strip[x]))

        for start, stop in ranges:
            grouped(start, stop, group_of(stop - start), plane)
        if write_strip:
            for start, stop in ranges:
                grouped(start, stop, GROUP_STRIPS, side)


class Only:
    def __init__(self, ref):
        self.ref = ref

    def __getitem__(self, index):
        return self.ref[index[1:]]


def final(new, k, was):
    return jnp.where(k > 0, new / jnp.maximum(k, 0.5), was)


def inner(*refs, first, last, deep):
    refs = list(refs)
    take = lambda n: [refs.pop(0) for _ in range(n)]
    flags, diffusion, own, strips, ylo, yhi = take(6)
    if not first:
        given = take(6)
    if last:
        (conc,) = take(1)
    part, out_edges, rows_lo, rows_hi, hist, hist_strip = take(6)
    if first:
        rock = take(6)
    a_main, b_main, a_strip, b_strip, edges, near = take(6)
    if not first:
        rock = take(3) + given[3:]
    if last:
        (was,) = take(1)
    (sems,) = take(1)

    def copy(src, dst):
        started.append(pltpu.make_async_copy(src, dst, sems.at[len(started)]))
        started[-1].start()
        return started[-1]

    started = []
    rows_y = pl.ds(ROW, NY)
    for f in range(2):
        copy(own.at[f], a_main.at[f, :, rows_y, :])
    if first:
        copy(own.at[2], rock[0].at[:, rows_y, :])
        copy(own.at[3], rock[2].at[:, rows_y, :])
    else:
        for i in range(3):
            copy(given[i], rock[i])
    if last:
        copy(conc, was)

    low_ok, high_ok = flags[2], flags[3]
    targets = [(0, a_main.at[0], a_strip.at[0]), (1, a_main.at[1], a_strip.at[1])]
    if first:
        targets += [(2, rock[0], rock[3]), (3, rock[2], rock[5])]
    for f, main, strip in targets:
        for x in range(NX):
            beyond = pl.ds(HALO * x, HALO)
            below, above = ylo[f, beyond, :] * low_ok, yhi[f, beyond, :] * high_ok
            place_plane(main, strip, x, None, below, above, strips[f, x])
    step = Step(diffusion, rock, near, edges)
    for item in started if first else started[:2]:
        item.wait()
    if first:
        step.weigh([(1, NX - 1)])

    def ready():
        for item in started[2:]:
            item.wait()

    back = []
    for s in range(1, deep + 1):
        src, dst = (a_main, b_main) if s % 2 else (b_main, a_main)
        src_strip, dst_strip = (a_strip, b_strip) if s % 2 else (b_strip, a_strip)
        half = (NX - 2 * s) // 2
        dots = [[(f, s + i * half, half)] for f in range(2) for i in range(2)]

        def write(x, t, new, k):
            for f in range(2):
                value = new[f]
                if s == deep and last:
                    value = final(value, k, was[f, x, 8 * t - 8 : 8 * t, :])
                dst[f, x, 8 + 8 * t : 16 + 8 * t, :] = value

        def write_strip(x, new):
            for f in range(2):
                dst_strip[f, x] = new[f]

        hook = ready if s == 1 and not first else None
        step.run(src, src_strip, [(s, NX - s)], dots, write, write_strip if s < deep else None, hook)
        if s < deep:
            for side, x in enumerate((s, NX - 2 - s)):
                back.append(copy(dst.at[:, pl.ds(x, 2), pl.ds(8, 8 * TILES), :], hist.at[s - 1, side]))
                for i in range(2):
                    for f in range(2):
                        hist_strip[s - 1, side, f, i] = dst_strip[f, x + i]
        else:
            middle = pl.ds(deep, NX - 2 * deep)
            back.append(copy(dst.at[:, middle, rows_y, :], part.at[:, middle]))
    if not last:
        for f in range(2):
            out_edges[f] = edges[f]
            for x in range(deep, NX - deep):
                rows_lo[f, HALO * x : HALO * (x + 1), :] = dst[f, x, ROW : ROW + HALO, :]
                rows_hi[f, HALO * x : HALO * (x + 1), :] = dst[f, x, ROW + NY - HALO : ROW + NY, :]
    for item in back:
        item.wait()


SHELL = 4 * HALO + 4


def outer(*refs, first, last, deep):
    refs = list(refs)
    take = lambda n: [refs.pop(0) for _ in range(n)]
    flags, diffusion, strips, ylo, yhi, own_lo, own_hi, xlo, xhi, hist, hist_strip, _ = take(12)
    in_edges, in_rows_lo, in_rows_hi = take(3)
    given = take(6)
    if last:
        (conc,) = take(1)
    if first:
        rock_lo, rock_hi, rock_lo_edge, rock_hi_edge = take(4)
    (out,) = take(1)
    if not last:
        out_xlo, out_xhi, right, left, rows_lo, rows_hi = take(6)
    if first:
        rock = take(6)
    a_main, b_main, a_strip, b_strip, edges, near = take(6)
    if not first:
        rock = take(3) + given[3:]
    if last:
        out_xlo, out_xhi, was = take(3)
    all_edges, sems = take(2)

    low_ok, high_ok = flags[2], flags[3]
    first_own, after_own = HALO, SHELL - HALO
    started = []

    def copy(src, dst):
        started.append(pltpu.make_async_copy(src, dst, sems.at[len(started)]))
        started[-1].start()
        return started[-1]

    if first:
        for i in range(3):
            copy(given[i].at[0:6], rock[i].at[HALO : HALO + 6])
            copy(given[i].at[NX - 6 : NX], rock[i].at[after_own - 6 : after_own])
        for i in range(3, 6):
            rock[i][HALO : HALO + 6] = given[i][0:6]
            rock[i][after_own - 6 : after_own] = given[i][NX - 6 : NX]
    else:
        for i in range(3):
            copy(given[i], rock[i])
    if last:
        copy(conc.at[:, 0:deep], was.at[:, 0:deep])
        copy(conc.at[:, NX - deep : NX], was.at[:, deep : 2 * deep])
    for s in range(1, deep):
        main, strip = (b_main, b_strip) if s % 2 else (a_main, a_strip)
        for side, to in enumerate((first_own + s, after_own - 2 - s)):
            copy(hist.at[s - 1, side], main.at[:, pl.ds(to, 2), pl.ds(8, 8 * TILES), :])
            for i in range(2):
                for f in range(2):
                    strip[f, to + i] = hist_strip[s - 1, side, f, i]
    for f in range(2):
        for i in range(2):
            low, high = own_lo[f, i], own_hi[f, own_hi.shape[1] - 1 - i]
            for tile, x, to in ((low, i, first_own + i), (high, NX - 1 - i, after_own - 1 - i)):
                beyond = pl.ds(HALO * x, HALO)
                below, above = ylo[f, beyond, :] * low_ok, yhi[f, beyond, :] * high_ok
                place_plane(a_main.at[f], a_strip.at[f], to, tile, below, above, strips[f, x])
    targets = [(0, a_main.at[0], a_strip.at[0]), (1, a_main.at[1], a_strip.at[1])]
    if first:
        targets += [(2, rock[0], rock[3]), (3, rock[2], rock[5])]
    for f, main, strip in targets:
        for d, (at_own, at_strip, at_below, at_above, more) in enumerate(message(deep)[0], 1):
            spans = ((at_below, more), (at_above, more), (at_strip, 8))
            for side, to, ok in ((0, first_own - d, flags[0]), (1, after_own - 1 + d, flags[1])):
                if f < 2:
                    slab, i = (xlo, xhi)[side], f
                    block = slab[i, at_own : at_own + NY] * ok
                else:
                    slab, i = (rock_lo_edge, rock_hi_edge)[side], f - 2
                    block = (rock_lo[i, deep - d] if side == 0 else rock_hi[i, d - 1]) * ok
                rest = [slab[i, at : at + n] * ok if more else None for at, n in spans]
                place_plane(main, strip, to, block, *rest)
    step = Step(diffusion, rock, near, edges)
    for item in started:
        item.wait()
    if first:
        step.weigh([(1, first_own + 1), (after_own - 1, SHELL - 1)])

    for s in range(1, deep + 1):
        src, dst = (a_main, b_main) if s % 2 else (b_main, a_main)
        src_strip, dst_strip = (a_strip, b_strip) if s % 2 else (b_strip, a_strip)
        ranges = [(first_own - deep + s, first_own + s), (after_own - s, after_own + deep - s)]
        dots = [[(f, start, deep) for f in range(2) for start, _ in ranges]]

        def write(x, t, new, k):
            for f in range(2):
                if s < deep:
                    dst[f, x, 8 + 8 * t : 16 + 8 * t, :] = new[f]
                else:
                    here = pl.ds(8 * t - 8, 8)
                    slab, at = (out_xlo, x - first_own) if side == 0 else (out_xhi, x - (after_own - deep))
                    value = final(new[f], k, was[f, at + deep * side, here, :]) if last else new[f]
                    slab[f, at, here, :] = value

        def write_strip(x, new):
            for f in range(2):
                dst_strip[f, x] = new[f]

        if s < deep:
            step.run(src, src_strip, ranges, dots, write, write_strip)
        else:
            for side in range(2):
                step.run(src, src_strip, ranges[side : side + 1], [] if side else dots, write)

    back = [copy(out_xlo, out.at[:, 0:deep]), copy(out_xhi, out.at[:, NX - deep : NX])]
    if not last:
        for f in range(2):
            all_edges[f] = in_edges[f]
            all_edges[f, 0:deep] = edges[f, first_own : first_own + deep]
            all_edges[f, NX - deep : NX] = edges[f, after_own - deep : after_own]
            rows_lo[f] = in_rows_lo[f]
            rows_hi[f] = in_rows_hi[f]
            for slab, x0 in ((out_xlo, 0), (out_xhi, NX - deep)):
                for d in range(deep):
                    there = pl.ds(HALO * (x0 + d), HALO)
                    rows_lo[f, there, :] = slab[f, d, 0:HALO, :]
                    rows_hi[f, there, :] = slab[f, d, NY - HALO : NY, :]
        pack_strips(all_edges, right, left, 2)
    for item in back:
        item.wait()


def group_of(planes):
    return planes if planes < 7 else 4


def grouped(start, stop, size, work):
    size = min(size, stop - start)

    def several(i, _):
        first = jnp.minimum(start + i * size, stop - size)
        for j in range(size):
            work(first + j)
        return 0

    lax.fori_loop(0, -(-(stop - start) // size), several, 0)


def call(kernel, outs, scratch, args, smem, name, any_in=(), any_out=(), aliases={}, flops=0, limit=16):
    f32 = lambda shape: jax.ShapeDtypeStruct(shape, jnp.float32)
    in_specs = [SMEM if i < smem else ANY if i in any_in else VMEM for i in range(len(args))]
    return pl.pallas_call(
        kernel,
        out_shape=[f32(shape) for shape in outs],
        in_specs=in_specs,
        out_specs=[ANY if i in any_out else VMEM for i in range(len(outs))],
        scratch_shapes=[pltpu.VMEM(shape, jnp.float32) if isinstance(shape, tuple) else shape for shape in scratch],
        input_output_aliases=aliases,
        cost_estimate=pl.CostEstimate(flops=flops, bytes_accessed=1 << 20, transcendentals=0) if flops else None,
        compiler_params=pltpu.CompilerParams(vmem_limit_bytes=limit * MIB),
        name=name,
    )(*args)


def call_prepare(outs, args):
    f32 = lambda shape: jax.ShapeDtypeStruct(shape, jnp.float32)
    part = pl.BlockSpec((SOME, NY, NZ), lambda i: (i, 0, 0))
    several = lambda count: pl.BlockSpec((count, SOME, NY, NZ), lambda i: (0, i, 0, 0))
    whole = lambda shape: pl.BlockSpec(shape, lambda i: (0,) * len(shape))
    line = pl.BlockSpec((4, SOME * HALO, NZ), lambda i: (0, i, 0))
    return pl.pallas_call(
        prepare,
        grid=(NX // SOME,),
        out_shape=[f32(shape) for shape in outs],
        in_specs=[several(2)] + [part] * 3,
        out_specs=[several(4)] + [whole(shape) for shape in outs[1:7]] + [line] * 2,
        scratch_shapes=[pltpu.VMEM((4, NX, 8, 128), jnp.float32)],
        compiler_params=pltpu.CompilerParams(vmem_limit_bytes=60 * MIB),
        name="prepare",
    )(*args)


def rock_shapes(planes):
    return [(planes, YF, NZ)] * 3 + [(planes, 8, 128)] * 3


def scratch_shapes(planes):
    return [(2, planes, YF, NZ)] * 2 + [(2, planes, 8, 128)] * 3 + [(2, planes, 8 * TILES, NZ)]


def shards(concentrations, pore, permeability, rate, diffusion):
    place = []
    for axis in ("gx", "gy", "gz"):
        index = lax.axis_index(axis)
        place += [index > 0, index < lax.axis_size(axis) - 1]
    flags = jnp.stack(place).astype(jnp.float32)

    slabs = lambda count, deep: [(count, deep, NY, NZ)] * 2
    messages = lambda count: [(count, NX // 2, 8, 128)] * 2 + [(count, NX * HALO, NZ)] * 2
    own, xlo, xhi, rock_lo, rock_hi, right, left, rows_lo, rows_hi = call_prepare(
        [(4, NX, NY, NZ)] + slabs(2, ROUNDS[0]) * 2 + messages(4), (concentrations, pore, permeability, rate)
    )
    ahead = (ring(rock_hi, "gx", 1), ring(rock_lo, "gx", -1))
    rock_in = rock_out = ()
    for turn, deep in enumerate(ROUNDS):
        first, last = turn == 0, turn == len(ROUNDS) - 1
        count = 4 if first else 2
        from_left, from_right = ring(right, "gz", 1), ring(left, "gz", -1)
        strips, ylo, yhi = call(
            functools.partial(strips_in, count=count),
            [(count, NX, 8, 128)] + [(count, NX * HALO + 32, NZ)] * 2,
            [],
            (flags, rows_lo, rows_hi, from_left, from_right),
            1,
            "strips_in",
        )
        from_ylo, from_yhi = ring(yhi, "gy", 1), ring(ylo, "gy", -1)
        strips, to_lo, to_hi, *rest = call(
            functools.partial(strips_all, count=count, deep=deep),
            [(count, NX, 8, 128)] + [(2, message(deep)[2], NZ)] * 2 + [(2, message(deep)[1], NZ)] * (count - 2),
            [],
            (flags, strips, from_ylo, from_yhi, xlo, xhi),
            1,
            "strips_all",
        )
        from_xlo, from_xhi = ring(to_hi, "gx", 1), ring(to_lo, "gx", -1)
        if first:
            ahead += (ring(rest[1], "gx", 1), ring(rest[0], "gx", -1))

        args = (flags, diffusion, own, strips, from_ylo, from_yhi, *rock_in)
        any_in = [2] if first else [2, 6, 7, 8]
        if last:
            any_in += [len(args)]
            args += (concentrations,)
        outs = [(2, NX, NY, NZ), (2, NX, 8, 128)] + [(2, NX * HALO, NZ)] * 2
        outs += [(deep - 1, 2, 2, 2, 8 * TILES, NZ), (deep - 1, 2, 2, 2, 8, 128)]
        scratch = scratch_shapes(NX)
        if first:
            outs += rock_shapes(NX)
        else:
            scratch += rock_shapes(NX)[:3]
        if last:
            scratch += [(2, NX, NY, NZ)]
        scratch += [pltpu.SemaphoreType.DMA((24,))]
        part, edges, rows_lo, rows_hi, hist, hist_strip, *made = call(
            functools.partial(inner, first=first, last=last, deep=deep),
            outs,
            scratch,
            args,
            2,
            "inner",
            any_in,
            [0, 4],
            flops=1 << 34,
            limit=36,
        )
        if first:
            rock_in = tuple(made)

        args = (flags, diffusion, strips, from_ylo, from_yhi, xlo, xhi, from_xlo, from_xhi, hist, hist_strip, part)
        args += (edges, rows_lo, rows_hi)
        any_in = [9, 11, 15, 16, 17]
        args += rock_in if first else rock_out
        if last:
            any_in += [len(args)]
            args += (concentrations,)
        if first:
            args += ahead
        outs = [(2, NX, NY, NZ)]
        scratch = scratch_shapes(SHELL)
        if not first:
            scratch += rock_shapes(SHELL)[:3]
        if last:
            scratch += slabs(2, deep) + [(2, 2 * deep, NY, NZ)]
        else:
            outs += slabs(2, deep) + messages(2)
        if first:
            outs += rock_shapes(SHELL)
        scratch += [(2, NX, 8, 128), pltpu.SemaphoreType.DMA((24,))]
        results = call(
            functools.partial(outer, first=first, last=last, deep=deep),
            outs,
            scratch,
            args,
            2,
            "outer",
            any_in,
            [0],
            {11: 0},
            limit=OUTER_LIMIT,
        )
        if last:
            return results[0]
        own, xlo, xhi, right, left, rows_lo, rows_hi, *made = results
        if first:
            rock_out = tuple(made)


def solution(mesh):
    placed = (
        P(None, "gx", "gy", "gz"),
        P("gx", "gy", "gz"),
        P("gx", "gy", "gz"),
        P("gx", "gy", "gz"),
        P(),
    )
    return jax.shard_map(
        shards, mesh=mesh, in_specs=placed, out_specs=P(None, "gx", "gy", "gz"), check_vma=False
    )
```

```python
import functools

import jax
import jax.numpy as jnp
from jax import lax
from jax.experimental import pallas as pl
from jax.experimental.pallas import tpu as pltpu
from jax.sharding import PartitionSpec as P

STEPS = 16
ROUNDS = (6, 5, 5)
HALO = 6
WIDE = 2 * HALO
NX, NY, NZ = 32, 64, 128
YF = NY + 32
ROW = 16
GROUP_STRIPS = 8
TILES = NY // 8 + 2
VMEM = pl.BlockSpec(memory_space=pltpu.VMEM)
SMEM = pl.BlockSpec(memory_space=pltpu.SMEM)
ANY = pl.BlockSpec(memory_space=pl.ANY)
MIB = 1024 * 1024
INNER_LIMIT, OUTER_LIMIT = 36, 32


def lanes():
    return lax.broadcasted_iota(jnp.int32, (8, 128), 1)


def groups():
    lane = lanes()
    group = row_tile(lane)
    return group, lane - WIDE * group


def row_tile(lane):
    return (lane * -(-4096 // WIDE)) >> 12


def rows():
    return lax.broadcasted_iota(jnp.int32, (8, 128), 0)


def roll(tile, shift, axis=1):
    size = tile.shape[axis]
    shift = shift % size
    return pltpu.roll(tile, shift, axis) if shift else tile


def ring(block, axis, distance):
    size = lax.axis_size(axis)
    return lax.ppermute(block, axis, [(i, (i + distance) % size) for i in range(size)])


def split(block, terms):
    parts = []
    for _ in range(terms):
        part = block.astype(jnp.bfloat16)
        block = block - part.astype(jnp.float32)
        parts.append(part)
    return jnp.concatenate(parts, axis=-1)


def zeros_and_ones(kind, terms):
    i = lax.broadcasted_iota(jnp.int32, (128, 128), 0)
    j = lax.broadcasted_iota(jnp.int32, (128, 128), 1)
    ones = (i == j + 1) | (i + 1 == j) if kind == "near" else i + j == 2 * WIDE * row_tile(i) + WIDE - 1
    return jnp.concatenate([jnp.where(ones, 1.0, 0.0).astype(jnp.bfloat16)] * terms, axis=0)


def pack_strips(edges, right, left, fields):
    low = groups()[1] < HALO
    half = NX // 2
    back = zeros_and_ones("turn", 3)
    for f in range(fields):
        turned = jnp.dot(
            split(edges[f].reshape(NX * 8, 128), 3), back, preferred_element_type=jnp.float32
        ).reshape(NX, 8, 128)
        for x in range(half):
            near, far = turned[x], turned[x + half]
            right[f, x] = jnp.where(low, roll(far, -HALO), near)
            left[f, x] = jnp.where(low, near, roll(far, HALO))


SOME = 4


def prepare(conc, pore, perm, rate, fields, xlo, xhi, rock_lo, rock_hi, right, left, rows_lo, rows_hi, edges):
    group = groups()[0]
    deep = ROUNDS[0]
    turn = pl.program_id(0)

    for x in range(SOME):
        strip = [jnp.zeros((8, 128), jnp.float32)] * 4
        for t in range(1, 9):
            here = pl.ds(8 * (t - 1), 8)
            solid = pore[x, here, :].astype(jnp.float32)
            k = solid * perm[x, here, :]
            r = solid * rate[x, here, :]
            for f, value in enumerate((k * conc[0, x, here, :], k * conc[1, x, here, :], k, r)):
                fields[f, x, here, :] = value
                strip[f] = jnp.where(group == t, roll(value, WIDE * t + HALO), strip[f])
        for f in range(4):
            edges[f, SOME * turn + x] = strip[f]
            rows_lo[f, HALO * x : HALO * (x + 1), :] = fields[f, x, 0:HALO, :]
            rows_hi[f, HALO * x : HALO * (x + 1), :] = fields[f, x, NY - HALO : NY, :]

    for out, rock, first in ((xlo, rock_lo, 0), (xhi, rock_hi, NX - deep)):
        for d in range(deep):
            there, here = divmod(first + d, SOME)

            @pl.when(turn == there)
            def _():
                for f in range(2):
                    out[f, d] = fields[f, here]
                    rock[f, d] = fields[f + 2, here]

    @pl.when(turn == NX // SOME - 1)
    def _():
        pack_strips(edges, right, left, 4)


def strips_in(flags, rows_lo, rows_hi, from_left, from_right, strips, ylo, yhi, *, count):
    group, place = groups()
    low = place < HALO
    left_ok, right_ok = flags[4], flags[5]
    half = NX // 2
    for f in range(count):
        for x in range(half):
            before, after = from_left[f, x] * left_ok, from_right[f, x] * right_ok
            strips[f, x] = jnp.where(low, after, before)
            strips[f, x + half] = jnp.where(low, roll(after, -HALO), roll(before, HALO))
        ylo[f, 0 : NX * HALO] = rows_lo[f]
        yhi[f, 0 : NX * HALO] = rows_hi[f]
        for some in range(4):
            first = last = jnp.zeros((8, 128), jnp.float32)
            for i in range(8):
                strip = strips[f, some * 8 + i]
                mine = group == i
                first = jnp.where(mine, roll(strip, WIDE * (i - 1)), first)
                last = jnp.where(mine, roll(strip, WIDE * (i - 8)), last)
            at = NX * HALO + 8 * some
            ylo[f, at : at + 8] = first
            yhi[f, at : at + 8] = last


def message(deep):
    edge = 8 * (deep - 1) + deep * (deep - 1)
    edge = -(-edge // 8) * 8
    at = 8 * (deep - 1)
    parts = []
    for d in range(1, deep + 1):
        more = deep - d
        parts.append((edge + NY * (d - 1), 8 * (d - 1), at, at + more, more))
        at += 2 * more
    return parts, edge, edge + NY * deep


def field_at(f, deep):
    _, edge, whole = message(deep)
    return f * whole if f < 2 else 2 * whole + (f - 2) * edge


def strips_all(flags, own, from_low, from_high, xlo, xhi, strips, *outs, count, deep):
    group, row = groups()[0], rows()
    low_ok, high_ok = flags[2], flags[3]
    under = (group == 0) & (row >= 8 - HALO)
    over = (group == 9) & (row < HALO)
    for f in range(count):
        for some in range(4):
            at = NX * HALO + 8 * some
            below = from_low[f, at : at + 8] * low_ok
            above = from_high[f, at : at + 8] * high_ok
            for i in range(8):
                x = some * 8 + i
                strip = jnp.where(under, roll(below, -WIDE * i), own[f, x])
                strips[f, x] = jnp.where(over, roll(above, WIDE * (9 - i)), strip)
        for d, (at_own, at_strip, at_below, at_above, more) in enumerate(message(deep)[0], 1):
            for side, slab, x in ((0, xlo, d - 1), (1, xhi, NX - d)):
                out, at = outs[side], field_at(f, deep)
                if f < 2:
                    out[at + at_own : at + at_own + NY] = slab[f, d - 1 if side == 0 else slab.shape[1] - d]
                if more:
                    low, high = HALO * (x + 1) - more, HALO * x
                    out[at + at_strip : at + at_strip + 8] = strips[f, x]
                    out[at + at_below : at + at_below + more] = from_low[f, low : low + more] * low_ok
                    out[at + at_above : at + at_above + more] = from_high[f, high : high + more] * high_ok


def place_plane(main, strip, to, block, below, above, side):
    if block is not None:
        main[to, ROW : ROW + NY, :] = block
    if below is not None:
        more = below.shape[0]
        main[to, ROW - more : ROW, :] = below
        main[to, ROW + NY : ROW + NY + more, :] = above
        strip[to] = side


def near_z(src, sums, pieces, near):
    blocks = [src[f, pl.ds(x, n), 8 : 8 + 8 * TILES, :].reshape(n * 8 * TILES, NZ) for f, x, n in pieces]
    block = jnp.concatenate(blocks, axis=0) if len(blocks) > 1 else blocks[0]
    total = jnp.dot(split(block, 2), near, preferred_element_type=jnp.float32)
    at = 0
    for f, x, n in pieces:
        sums[f, pl.ds(x, n)] = total[at : at + n * 8 * TILES].reshape(n, 8 * TILES, NZ)
        at += n * 8 * TILES


def ends_z(strip, t, ends):
    return jnp.where(ends, roll(strip, -(WIDE * t + HALO)), 0.0)


def near_xy(main, x, t):
    at = 8 + 8 * t
    rows_y = main[x, at - 1 : at + 7, :] + main[x, at + 1 : at + 9, :]
    rows_x = main[x - 1, at : at + 8, :] + main[x + 1, at : at + 8, :]
    return rows_y + rows_x


def near_sum_strip(strip, x, edge, place, row):
    here = strip[x]
    left = jnp.where(place == HALO, edge, roll(here, 1))
    right = jnp.where(place == HALO - 1, edge, roll(here, -1))
    up = roll(here, -1, 0)
    up = jnp.where(row == 7, roll(up, -WIDE), up)
    down = roll(here, 1, 0)
    down = jnp.where(row == 0, roll(down, WIDE), down)
    return (up + down) + (strip[x - 1] + strip[x + 1]) + (left + right), here


def react_step(d0, d1, u0, u1, s0, s1, k, g, r):
    kk = k * k
    over = jnp.maximum(k + u0, 0.5)
    inverse = pl.reciprocal(over, approx=True)
    inverse = inverse * (2.0 - over * inverse)
    q = (r * u0) * (u0 * inverse)
    n0 = u0 + (d0 * (kk * s0 - g * u0) - q)
    n1 = u1 + (d1 * (kk * s1 - g * u1) + q)
    return n0, n1


class Step:
    def __init__(self, diffusion, rock, near, edges):
        lane, self.row = lanes(), rows()
        self.group, self.place = groups()
        self.zero = jnp.zeros((8, 128), jnp.float32)
        self.ends = (lane == 0) | (lane == 127)
        self.beside = zeros_and_ones("near", 2)
        self.d = diffusion[0], diffusion[1]
        self.k, self.g, self.r, self.k_strip, self.g_strip, self.r_strip = rock
        self.near, self.edges = near, edges

    def into(self, edge, t, tile):
        return jnp.where(self.group == t, roll(tile, WIDE * t + HALO), edge)

    def weigh(self, ranges):
        def plane(x):
            edge, strip = self.zero, self.k_strip[x]
            for t in range(TILES):
                at = pl.ds(8 + 8 * t, 8)
                here = self.k[x, at, :]
                total = near_xy(self.k, x, t) + (self.near[0, x, 8 * t : 8 * t + 8, :] + ends_z(strip, t, self.ends))
                self.g[x, at, :] = here * total
                edge = self.into(edge, t, here)
            self.edges[0, x] = edge

        def side(x):
            total, here = near_sum_strip(self.k_strip, x, self.edges[0, x], self.place, self.row)
            self.g_strip[x] = here * total

        for start, stop in ranges:
            near_z(Only(self.k), self.near, [(0, start, stop - start)], self.beside)
            grouped(start, stop, group_of(stop - start), plane)
            grouped(start, stop, GROUP_STRIPS, side)

    def run(self, src, src_strip, ranges, dots, write, write_strip=None):
        tiles = range(TILES) if write_strip else range(1, TILES - 1)
        for pieces in dots:
            near_z(src, self.near, pieces, self.beside)

        def plane(x):
            edge, strip = [self.zero] * 2, [src_strip[0, x], src_strip[1, x]]
            for t in tiles:
                at = pl.ds(8 + 8 * t, 8)
                u = [src[f, x, at, :] for f in range(2)]
                total = [
                    near_xy(src.at[f], x, t) + (self.near[f, x, 8 * t : 8 * t + 8, :] + ends_z(strip[f], t, self.ends))
                    for f in range(2)
                ]
                k = self.k[x, at, :]
                new = react_step(*self.d, *u, *total, k, self.g[x, at, :], self.r[x, at, :])
                write(x, t, new, k)
                for f in range(2):
                    edge[f] = self.into(edge[f], t, u[f] if write_strip else new[f])
            for f in range(2):
                self.edges[f, x] = edge[f]

        def side(x):
            both = [near_sum_strip(src_strip.at[f], x, self.edges[f, x], self.place, self.row) for f in range(2)]
            total, u = zip(*both)
            write_strip(x, react_step(*self.d, *u, *total, self.k_strip[x], self.g_strip[x], self.r_strip[x]))

        for start, stop in ranges:
            grouped(start, stop, group_of(stop - start), plane)
        if write_strip:
            for start, stop in ranges:
                grouped(start, stop, GROUP_STRIPS, side)


class Only:
    def __init__(self, ref):
        self.ref = ref

    def __getitem__(self, index):
        return self.ref[index[1:]]


def final(new, k, was):
    return jnp.where(k > 0, new / jnp.maximum(k, 0.5), was)


def inner(*refs, first, last, deep):
    refs = list(refs)
    take = lambda n: [refs.pop(0) for _ in range(n)]
    flags, diffusion, own, strips, ylo, yhi = take(6)
    if not first:
        rock = take(6)
    if last:
        (conc,) = take(1)
    part, out_edges, rows_lo, rows_hi, hist, hist_strip = take(6)
    if first:
        rock = take(6)
    a_main, b_main, a_strip, b_strip, edges, near = take(6)

    low_ok, high_ok = flags[2], flags[3]
    targets = [(0, a_main.at[0], a_strip.at[0]), (1, a_main.at[1], a_strip.at[1])]
    if first:
        targets += [(2, rock[0], rock[3]), (3, rock[2], rock[5])]
    for f, main, strip in targets:
        for x in range(NX):
            beyond = pl.ds(HALO * x, HALO)
            below, above = ylo[f, beyond, :] * low_ok, yhi[f, beyond, :] * high_ok
            place_plane(main, strip, x, own[f, x], below, above, strips[f, x])
    step = Step(diffusion, rock, near, edges)
    if first:
        step.weigh([(1, NX - 1)])

    for s in range(1, deep + 1):
        src, dst = (a_main, b_main) if s % 2 else (b_main, a_main)
        src_strip, dst_strip = (a_strip, b_strip) if s % 2 else (b_strip, a_strip)
        half = (NX - 2 * s) // 2
        dots = [[(f, s + i * half, half)] for f in range(2) for i in range(2)]

        def write(x, t, new, k):
            for f in range(2):
                if s < deep:
                    dst[f, x, 8 + 8 * t : 16 + 8 * t, :] = new[f]
                else:
                    here = pl.ds(8 * t - 8, 8)
                    part[f, x, here, :] = final(new[f], k, conc[f, x, here, :]) if last else new[f]

        def write_strip(x, new):
            for f in range(2):
                dst_strip[f, x] = new[f]

        step.run(src, src_strip, [(s, NX - s)], dots, write, write_strip if s < deep else None)
        if s < deep:
            for side, x in enumerate((s, NX - 2 - s)):
                for i in range(2):
                    for f in range(2):
                        hist[s - 1, side, f, i] = dst[f, x + i, 8 : 8 + 8 * TILES, :]
                        hist_strip[s - 1, side, f, i] = dst_strip[f, x + i]
    if not last:
        for f in range(2):
            out_edges[f] = edges[f]
            for x in range(deep, NX - deep):
                rows_lo[f, HALO * x : HALO * (x + 1), :] = part[f, x, 0:HALO, :]
                rows_hi[f, HALO * x : HALO * (x + 1), :] = part[f, x, NY - HALO : NY, :]


SHELL = 4 * HALO + 4


def outer(*refs, first, last, deep):
    refs = list(refs)
    take = lambda n: [refs.pop(0) for _ in range(n)]
    flags, diffusion, strips, ylo, yhi, own_lo, own_hi, xlo, xhi, hist, hist_strip, part = take(12)
    in_edges, in_rows_lo, in_rows_hi = take(3)
    given = take(6)
    if last:
        (conc,) = take(1)
    if first:
        rock_lo, rock_hi = take(2)
    (out,) = take(1)
    if not last:
        out_xlo, out_xhi, right, left, rows_lo, rows_hi = take(6)
    if first:
        rock = take(6)
    a_main, b_main, a_strip, b_strip, edges, near = take(6)
    if not first:
        rock = given
    if last:
        out_xlo, out_xhi, was = take(3)
    all_edges, sems = take(2)

    low_ok, high_ok = flags[2], flags[3]
    first_own, after_own = HALO, SHELL - HALO
    started = []
    if last:
        for i, x in enumerate((0, NX - deep)):
            item = pltpu.make_async_copy(conc.at[:, x : x + deep], was.at[:, deep * i : deep * (i + 1)], sems.at[i])
            item.start()
            started.append(item)
    if first:
        for i in range(6):
            rock[i][HALO : HALO + 6] = given[i][0:6]
            rock[i][after_own - 6 : after_own] = given[i][NX - 6 : NX]
    for s in range(1, deep):
        main, strip = (b_main, b_strip) if s % 2 else (a_main, a_strip)
        for side, to in enumerate((first_own + s, after_own - 2 - s)):
            for i in range(2):
                for f in range(2):
                    main[f, to + i, 8 : 8 + 8 * TILES, :] = hist[s - 1, side, f, i]
                    strip[f, to + i] = hist_strip[s - 1, side, f, i]
    for f in range(2):
        for i in range(2):
            low, high = own_lo[f, i], own_hi[f, own_hi.shape[1] - 1 - i]
            for tile, x, to in ((low, i, first_own + i), (high, NX - 1 - i, after_own - 1 - i)):
                beyond = pl.ds(HALO * x, HALO)
                below, above = ylo[f, beyond, :] * low_ok, yhi[f, beyond, :] * high_ok
                place_plane(a_main.at[f], a_strip.at[f], to, tile, below, above, strips[f, x])
    targets = [(0, a_main.at[0], a_strip.at[0]), (1, a_main.at[1], a_strip.at[1])]
    if first:
        targets += [(2, rock[0], rock[3]), (3, rock[2], rock[5])]
    for f, main, strip in targets:
        for d, (at_own, at_strip, at_below, at_above, more) in enumerate(message(deep)[0], 1):
            spans = ((at_below, more), (at_above, more), (at_strip, 8))
            for side, to, ok in ((0, first_own - d, flags[0]), (1, after_own - 1 + d, flags[1])):
                slab, at_field = (xlo, xhi)[side], field_at(f, deep)
                if f < 2:
                    block = slab[at_field + at_own : at_field + at_own + NY] * ok
                else:
                    block = (rock_lo[f - 2, deep - d] if side == 0 else rock_hi[f - 2, d - 1]) * ok
                rest = [slab[at_field + at : at_field + at + n] * ok if more else None for at, n in spans]
                place_plane(main, strip, to, block, *rest)
    step = Step(diffusion, rock, near, edges)
    for item in started:
        item.wait()
    if first:
        step.weigh([(1, first_own + 1), (after_own - 1, SHELL - 1)])

    for s in range(1, deep + 1):
        src, dst = (a_main, b_main) if s % 2 else (b_main, a_main)
        src_strip, dst_strip = (a_strip, b_strip) if s % 2 else (b_strip, a_strip)
        ranges = [(first_own - deep + s, first_own + s), (after_own - s, after_own + deep - s)]
        dots = [[(f, start, deep) for f in range(2) for start, _ in ranges]]

        def write(x, t, new, k):
            for f in range(2):
                if s < deep:
                    dst[f, x, 8 + 8 * t : 16 + 8 * t, :] = new[f]
                else:
                    here = pl.ds(8 * t - 8, 8)
                    slab, at = (out_xlo, x - first_own) if side == 0 else (out_xhi, x - (after_own - deep))
                    value = final(new[f], k, was[f, at + deep * side, here, :]) if last else new[f]
                    slab[f, at, here, :] = value

        def write_strip(x, new):
            for f in range(2):
                dst_strip[f, x] = new[f]

        if s < deep:
            step.run(src, src_strip, ranges, dots, write, write_strip)
        else:
            for side in range(2):
                step.run(src, src_strip, ranges[side : side + 1], [] if side else dots, write)

    for f in range(2):
        out[f, 0:deep] = out_xlo[f]
        out[f, deep : NX - deep] = part[f, deep : NX - deep]
        out[f, NX - deep : NX] = out_xhi[f]
    if not last:
        for f in range(2):
            all_edges[f] = in_edges[f]
            all_edges[f, 0:deep] = edges[f, first_own : first_own + deep]
            all_edges[f, NX - deep : NX] = edges[f, after_own - deep : after_own]
            rows_lo[f] = in_rows_lo[f]
            rows_hi[f] = in_rows_hi[f]
            for slab, x0 in ((out_xlo, 0), (out_xhi, NX - deep)):
                for d in range(deep):
                    there = pl.ds(HALO * (x0 + d), HALO)
                    rows_lo[f, there, :] = slab[f, d, 0:HALO, :]
                    rows_hi[f, there, :] = slab[f, d, NY - HALO : NY, :]
        pack_strips(all_edges, right, left, 2)


def group_of(planes):
    return planes if planes < 7 else 4


def grouped(start, stop, size, work):
    size = min(size, stop - start)

    def several(i, _):
        first = jnp.minimum(start + i * size, stop - size)
        for j in range(size):
            work(first + j)
        return 0

    lax.fori_loop(0, -(-(stop - start) // size), several, 0)


def call(kernel, outs, scratch, args, smem, name, any_in=(), flops=0, limit=16):
    f32 = lambda shape: jax.ShapeDtypeStruct(shape, jnp.float32)
    in_specs = [SMEM if i < smem else ANY if i in any_in else VMEM for i in range(len(args))]
    return pl.pallas_call(
        kernel,
        out_shape=[f32(shape) for shape in outs],
        in_specs=in_specs,
        out_specs=[VMEM] * len(outs),
        scratch_shapes=[pltpu.VMEM(shape, jnp.float32) if isinstance(shape, tuple) else shape for shape in scratch],
        cost_estimate=pl.CostEstimate(flops=flops, bytes_accessed=1 << 20, transcendentals=0) if flops else None,
        compiler_params=pltpu.CompilerParams(vmem_limit_bytes=limit * MIB),
        name=name,
    )(*args)


def call_prepare(outs, args):
    f32 = lambda shape: jax.ShapeDtypeStruct(shape, jnp.float32)
    part = pl.BlockSpec((SOME, NY, NZ), lambda i: (i, 0, 0))
    several = lambda count: pl.BlockSpec((count, SOME, NY, NZ), lambda i: (0, i, 0, 0))
    whole = lambda shape: pl.BlockSpec(shape, lambda i: (0,) * len(shape))
    line = pl.BlockSpec((4, SOME * HALO, NZ), lambda i: (0, i, 0))
    return pl.pallas_call(
        prepare,
        grid=(NX // SOME,),
        out_shape=[f32(shape) for shape in outs],
        in_specs=[several(2)] + [part] * 3,
        out_specs=[several(4)] + [whole(shape) for shape in outs[1:7]] + [line] * 2,
        scratch_shapes=[pltpu.VMEM((4, NX, 8, 128), jnp.float32)],
        compiler_params=pltpu.CompilerParams(vmem_limit_bytes=60 * MIB),
        name="prepare",
    )(*args)


def rock_shapes(planes):
    return [(planes, YF, NZ)] * 3 + [(planes, 8, 128)] * 3


def scratch_shapes(planes):
    return [(2, planes, YF, NZ)] * 2 + [(2, planes, 8, 128)] * 3 + [(2, planes, 8 * TILES, NZ)]


def shards(concentrations, pore, permeability, rate, diffusion):
    place = []
    for axis in ("gx", "gy", "gz"):
        index = lax.axis_index(axis)
        place += [index > 0, index < lax.axis_size(axis) - 1]
    flags = jnp.stack(place).astype(jnp.float32)

    slabs = lambda count, deep: [(count, deep, NY, NZ)] * 2
    messages = lambda count: [(count, NX // 2, 8, 128)] * 2 + [(count, NX * HALO, NZ)] * 2
    own, xlo, xhi, rock_lo, rock_hi, right, left, rows_lo, rows_hi = call_prepare(
        [(4, NX, NY, NZ)] + slabs(2, ROUNDS[0]) * 2 + messages(4), (concentrations, pore, permeability, rate)
    )
    ahead = (ring(rock_hi, "gx", 1), ring(rock_lo, "gx", -1))
    rock_in = rock_out = ()
    for turn, deep in enumerate(ROUNDS):
        first, last = turn == 0, turn == len(ROUNDS) - 1
        count = 4 if first else 2
        from_left, from_right = ring(right, "gz", 1), ring(left, "gz", -1)
        strips, ylo, yhi = call(
            functools.partial(strips_in, count=count),
            [(count, NX, 8, 128)] + [(count, NX * HALO + 32, NZ)] * 2,
            [],
            (flags, rows_lo, rows_hi, from_left, from_right),
            1,
            "strips_in",
        )
        from_ylo, from_yhi = ring(yhi, "gy", 1), ring(ylo, "gy", -1)
        strips, to_lo, to_hi = call(
            functools.partial(strips_all, count=count, deep=deep),
            [(count, NX, 8, 128)] + [(field_at(count, deep), NZ)] * 2,
            [],
            (flags, strips, from_ylo, from_yhi, xlo, xhi),
            1,
            "strips_all",
        )
        from_xlo, from_xhi = ring(to_hi, "gx", 1), ring(to_lo, "gx", -1)

        args = (flags, diffusion, own, strips, from_ylo, from_yhi, *rock_in)
        if last:
            args += (concentrations,)
        outs = [(2, NX, NY, NZ), (2, NX, 8, 128)] + [(2, NX * HALO, NZ)] * 2
        outs += [(deep - 1, 2, 2, 2, 8 * TILES, NZ), (deep - 1, 2, 2, 2, 8, 128)]
        scratch = scratch_shapes(NX)
        if first:
            outs += rock_shapes(NX)
        part, edges, rows_lo, rows_hi, hist, hist_strip, *made = call(
            functools.partial(inner, first=first, last=last, deep=deep),
            outs,
            scratch,
            args,
            2,
            "inner",
            flops=1 << 34,
            limit=INNER_LIMIT,
        )
        if first:
            rock_in = tuple(made)

        args = (flags, diffusion, strips, from_ylo, from_yhi, xlo, xhi, from_xlo, from_xhi, hist, hist_strip, part)
        args += (edges, rows_lo, rows_hi)
        any_in = []
        args += rock_in if first else rock_out
        if last:
            any_in += [len(args)]
            args += (concentrations,)
        if first:
            args += ahead
        outs = [(2, NX, NY, NZ)]
        scratch = scratch_shapes(SHELL)
        if last:
            scratch += slabs(2, deep) + [(2, 2 * deep, NY, NZ)]
        else:
            outs += slabs(2, deep) + messages(2)
        if first:
            outs += rock_shapes(SHELL)
        scratch += [(2, NX, 8, 128), pltpu.SemaphoreType.DMA((2,))]
        results = call(
            functools.partial(outer, first=first, last=last, deep=deep),
            outs,
            scratch,
            args,
            2,
            "outer",
            any_in,
            limit=OUTER_LIMIT,
        )
        if last:
            return results[0]
        own, xlo, xhi, right, left, rows_lo, rows_hi, *made = results
        if first:
            rock_out = tuple(made)


def solution(mesh):
    placed = (
        P(None, "gx", "gy", "gz"),
        P("gx", "gy", "gz"),
        P("gx", "gy", "gz"),
        P("gx", "gy", "gz"),
        P(),
    )
    return jax.shard_map(
        shards, mesh=mesh, in_specs=placed, out_specs=P(None, "gx", "gy", "gz"), check_vma=False
    )
```
